512 devices in a mesh: section: 128 (over z_hi, y, x, core), tensor: 4 (over z_lo).
Axes of the slice: x: 4, y: 8, z: 8 (z_hi: 2, z_lo: 4; z = z_hi * 4 + z_lo), core: 2. Of those that a mesh axis runs over, the one named last changes fastest.
Arguments:
- inputs: bfloat16 [32768, 6144], P('section', 'tensor'), may hold values from -6 to 6
- cotangent: bfloat16 [32768, 6144], P('section', 'tensor'), may hold values from -6 to 6
- ffn_weights: bfloat16 [3, 14336, 6144], P(None, 'section', 'tensor'), may hold values from -0.078125 to 0.078125
Outputs:
- input_grads: bfloat16 [32768, 6144], P('section', 'tensor')
- weight_grads: bfloat16 [3, 14336, 6144], P(None, 'section', 'tensor')
The draws below stay inside these ranges and needn't reach their ends.
All inputs are finite; a program needn't handle non-finite values.
Results may differ from the reference program's by a relative error of at most 0.0049.
Values may be sent and summed in bfloat16 or wider, within the bound.
A program may use at most 64 MiB of HBM per device.

```python
import jax
import jax.numpy as jnp
from jax import lax

D = 6144
FF = 14336
TOK_DEV = 256
HOPS = 4
TOKENS = 32768
N_SECTION = 128


def levels(stream_key, shape, shards, low, high):
    factor_of, own = 1.0, jax.random.fold_in(stream_key, 6)
    for dim, blocks in shards:
        heights = jnp.exp(jax.random.uniform(jax.random.fold_in(own, dim), (blocks,), jnp.float32, low / len(shards), high / len(shards)))
        factor_of = factor_of * jnp.repeat(heights, shape[dim] // blocks).reshape([-1 if axis == dim else 1 for axis in range(len(shape))])
    return factor_of


def normal_values(own_key, dims, scale, most, shards=(), kind=jnp.bfloat16):
    entries = scale * jax.random.normal(own_key, dims, jnp.float32)
    if shards:
        entries = entries * levels(own_key, dims, shards, -0.22, 0.18)
    return jnp.clip(entries, -most, most).astype(kind)


def setup_inputs(seed: int = 0) -> dict:
    streams_of = jax.random.split(jax.random.key(seed), 4)
    inputs = normal_values(streams_of[0], (TOKENS, D), 1.0, 6.0, ((0, 128), (1, 4)))
    cotangent = normal_values(streams_of[1], (TOKENS, D), 1.0, 6.0, ((0, 128), (1, 4)))
    ffn_weights = normal_values(streams_of[2], (3, FF, D), D ** -0.5, 0.078125, ((1, 128), (2, 4)))
    return dict(inputs=inputs, cotangent=cotangent, ffn_weights=ffn_weights)


def reference(inputs, cotangent, ffn_weights):
    width = FF // N_SECTION
    blocks = ffn_weights.reshape(3, N_SECTION, width, D)

    def visit(totals, section_index):
        rows_x = lax.dynamic_slice_in_dim(inputs, section_index * TOK_DEV, TOK_DEV, 0).astype(jnp.float32)
        rows_dy = lax.dynamic_slice_in_dim(cotangent, section_index * TOK_DEV, TOK_DEV, 0).astype(jnp.float32)
        partial_sums = jnp.zeros((TOK_DEV, D), jnp.float32)
        for hop_index in range(HOPS):
            owner = ((section_index - hop_index) % N_SECTION).astype(jnp.int32)
            weights_here = lax.dynamic_index_in_dim(blocks, owner, 1, keepdims=False).astype(jnp.float32)
            gate_value = jnp.einsum("rd,hd->rh", rows_x, weights_here[0])
            up_value = jnp.einsum("rd,hd->rh", rows_x, weights_here[1])
            sigmoid_gate = jax.nn.sigmoid(gate_value)
            silu_gate = gate_value * sigmoid_gate
            hidden = (silu_gate * up_value).astype(jnp.bfloat16).astype(jnp.float32)
            hidden_grad = jnp.einsum("rd,hd->rh", rows_dy, weights_here[2])
            up_grad = (hidden_grad * silu_gate).astype(jnp.bfloat16).astype(jnp.float32)
            gate_grad = (hidden_grad * up_value * sigmoid_gate * (1.0 + gate_value * (1.0 - sigmoid_gate))).astype(jnp.bfloat16).astype(jnp.float32)
            terms = jnp.stack([
                jnp.einsum("rh,rd->hd", gate_grad, rows_x),
                jnp.einsum("rh,rd->hd", up_grad, rows_x),
                jnp.einsum("rh,rd->hd", hidden, rows_dy)])
            current = lax.dynamic_index_in_dim(totals, owner, 1, keepdims=True)
            totals = lax.dynamic_update_index_in_dim(totals, current + terms[:, None], owner, 1)
            partial_sums = partial_sums + jnp.einsum("rh,hd->rd", gate_grad, weights_here[0]) + jnp.einsum("rh,hd->rd", up_grad, weights_here[1])
        return totals, partial_sums.astype(jnp.bfloat16)

    start = jnp.zeros((3, N_SECTION, width, D), jnp.float32)
    totals, rows_out = lax.scan(visit, start, jnp.arange(N_SECTION, dtype=jnp.int32))
    return rows_out.reshape(N_SECTION * TOK_DEV, D), totals.reshape(3, FF, D).astype(jnp.bfloat16)
```

```python
import functools

import jax
import jax.numpy as jnp
from jax import lax
from jax.experimental import pallas as pl
from jax.experimental.pallas import tpu as pltpu
from jax.sharding import PartitionSpec as P

MESH = pl.DeviceIdType.MESH
F32 = jnp.float32
BF16 = jnp.bfloat16

W_MATE, W_NEXT, W_NEXT_BACK, W_LAST, W_LAST_BACK, X_BACK, Y_BACK, PART_A, PART_B, DW_BACK, DX_NEXT = range(11)


def dot_nt(a, b):
    return lax.dot_general(a, b, (((1,), (1,)), ((), ())), preferred_element_type=F32)


def dot_nn(a, b):
    return jnp.dot(a, b, preferred_element_type=F32)


def kernel(
    n_section, n_tensor, tile,
    x_ref, y_ref, wt_ref, gx_ref, gw_ref,
    w, xf, yf, part, rs_out, rs_in, ag, agt, dw0, dxa, pa, pb, ca, dxf, sp, sc, sx,
    msg_s, msg_r, rs_s, rs_r, ag_s, ag_r,
):
    section, me_t = lax.axis_index("section"), lax.axis_index("tensor")
    even = lax.rem(section, 2) == 0
    odd = jnp.logical_not(even)
    tokens, depth = x_ref.shape
    height, padded = wt_ref.shape[1], w.shape[2]
    rows = tokens // n_tensor

    def at(by):
        return (lax.rem(section + by + n_section, n_section), me_t)

    def peer(by):
        return (section, lax.rem(me_t + by, n_tensor))

    def rows_of(t):
        return pl.ds(pl.multiple_of(t * rows, rows), rows)

    def message(kind, src, dst, to):
        return pltpu.make_async_remote_copy(
            src_ref=src, dst_ref=dst, send_sem=msg_s.at[kind], recv_sem=msg_r.at[kind],
            device_id=to, device_id_type=MESH,
        )

    def slot(i):
        return w.at[i, :, pl.ds(0, height), :]

    w_mate = message(W_MATE, wt_ref, slot(3), at(1))
    w_next = message(W_NEXT, wt_ref, slot(1), at(3))
    w_next_back = message(W_NEXT_BACK, slot(1), slot(1), at(-1))
    w_last = message(W_LAST, wt_ref, slot(2), at(1))
    w_last_back = message(W_LAST_BACK, slot(2), slot(2), at(1))
    x_back = message(X_BACK, x_ref, xf, at(-2))
    y_back = message(Y_BACK, y_ref, yf, at(-2))
    part_a_even = message(PART_A, sp.at[0], pa, at(1))
    part_a_odd = message(PART_A, sp.at[0], pa, at(-1))
    part_b = message(PART_B, sp.at[1], pb, at(-1))
    dw_back_even = message(DW_BACK, sc, ca, at(-1))
    dw_back_odd = message(DW_BACK, sc, ca, at(-3))
    dx_next = message(DX_NEXT, sx, dxf, at(2))

    barrier = pltpu.get_barrier_semaphore()

    def greet(to):
        pl.semaphore_signal(barrier, inc=1, device_id=to, device_id_type=MESH)

    for by in range(1, n_tensor):
        greet(peer(by))

    @pl.when(even)
    def _():
        for by in (1, -1, 3, -2, 2):
            greet(at(by))

    @pl.when(odd)
    def _():
        for by in (-1, 1, -3):
            greet(at(by))

    for i in range(4):
        w[i, :, height:, :] = jnp.zeros((3, padded - height, depth), BF16)
    w[0, :, :height, :] = wt_ref[...]

    @pl.when(even)
    def _():
        pl.semaphore_wait(barrier, n_tensor - 1 + 5)

    @pl.when(odd)
    def _():
        pl.semaphore_wait(barrier, n_tensor - 1 + 3)

    def rs_copy(st, by):
        return pltpu.make_async_remote_copy(
            src_ref=rs_out.at[st, rows_of(lax.rem(me_t + by, n_tensor))], dst_ref=rs_in.at[st, by - 1],
            send_sem=rs_s.at[st, by - 1], recv_sem=rs_r.at[st, by - 1],
            device_id=peer(by), device_id_type=MESH,
        )

    def ag_copy(st, by):
        return pltpu.make_async_remote_copy(
            src_ref=ag.at[st, rows_of(me_t)], dst_ref=ag.at[st, rows_of(me_t)],
            send_sem=ag_s.at[st, by - 1], recv_sem=ag_r.at[st, by - 1],
            device_id=peer(by), device_id_type=MESH,
        )

    def ag_arrival(st, by):
        src_t = lax.rem(me_t - by + n_tensor, n_tensor)
        return pltpu.make_async_remote_copy(
            src_ref=ag.at[st, rows_of(src_t)], dst_ref=ag.at[st, rows_of(src_t)],
            send_sem=ag_s.at[st, by - 1], recv_sem=ag_r.at[st, by - 1],
            device_id=peer(by), device_id_type=MESH,
        )

    def forward(st, x, y, i):
        gu = dot_nt(x[...], w[i, 0:2].reshape(2 * padded, depth))
        part[st, :, : 2 * padded] = gu
        rs_out[st, :, : 2 * padded] = gu.astype(BF16)
        d = dot_nt(y[...], w[i, 2])
        part[st, :, 2 * padded :] = d
        rs_out[st, :, 2 * padded :] = d.astype(BF16)
        for by in range(1, n_tensor):
            rs_copy(st, by).start()

    def middle(st):
        for by in range(1, n_tensor):
            rs_copy(st, by).wait_recv()
        own = rows_of(me_t)
        total = part[st, own, :]
        for by in range(1, n_tensor):
            total = total + rs_in[st, by - 1].astype(F32)
        g, u, dh = total[:, :padded], total[:, padded : 2 * padded], total[:, 2 * padded :]
        sig = jax.nn.sigmoid(g)
        silu = g * sig
        ag[st, own, :padded] = (dh * u * sig * (1.0 + g * (1.0 - sig))).astype(BF16)
        ag[st, own, padded : 2 * padded] = (dh * silu).astype(BF16)
        ag[st, own, 2 * padded :] = (silu * u).astype(BF16)
        for by in range(1, n_tensor):
            ag_copy(st, by).start()

    def gathered(st):
        for by in range(1, n_tensor):
            ag_arrival(st, by).wait_recv()
        agt[st] = ag[st].T

    def weight_terms(pairs, emit):
        @pl.loop(0, depth // tile)
        def _(j):
            cols = pl.ds(pl.multiple_of(j * tile, tile), tile)
            gu = sum(dot_nn(agt[st, : 2 * padded], x[:, cols]) for st, x, _ in pairs)
            emit(0, cols, gu[:height])
            emit(1, cols, gu[padded : padded + height])
            emit(2, cols, sum(dot_nn(agt[st, 2 * padded :], y[:, cols]) for st, _, y in pairs)[:height])

    def input_terms(pairs, emit):
        @pl.loop(0, depth // tile)
        def _(j):
            cols = pl.ds(pl.multiple_of(j * tile, tile), tile)
            emit(
                cols,
                sum(
                    dot_nn(ag[st, :, : 2 * padded], w[i, 0:2, :, cols].reshape(2 * padded, tile))
                    for st, i in pairs
                ),
            )

    def to_f32(ref):
        def emit(k, cols, value):
            ref[k, :, cols] = value

        return emit

    def to_bf16(ref):
        def emit(k, cols, value):
            ref[k, :, cols] = value.astype(BF16)

        return emit

    def dx_acc(cols, value):
        dxa[:, cols] = value

    @pl.when(even)
    def _():
        w_next.start()
        x_back.start()
        y_back.start()
        w_mate.start()
        forward(0, x_ref, y_ref, 0)
        middle(0)
        gathered(0)
        weight_terms([(0, x_ref, y_ref)], to_f32(dw0))
        w_next_back.wait_recv()
        forward(1, x_ref, y_ref, 1)
        middle(1)
        gathered(1)
        weight_terms([(1, x_ref, y_ref)], to_bf16(sp.at[0]))
        part_a_even.start()
        input_terms([(0, 0), (1, 1)], dx_acc)
        x_back.wait_recv()
        y_back.wait_recv()
        w_last.wait_recv()
        w_last_back.start()
        forward(3, xf, yf, 2)
        forward(2, x_ref, y_ref, 2)
        middle(3)
        middle(2)
        gathered(3)

        def dx_out(cols, value):
            sx[:, cols] = value.astype(BF16)

        input_terms([(3, 2)], dx_out)
        dx_next.start()
        gathered(2)

        def dw_f32(k, cols, value):
            part_dw = value
            sc[k, :, cols] = (part_dw + pb[k, :, cols].astype(F32)).astype(BF16)

        part_b.wait_recv()
        weight_terms([(2, x_ref, y_ref), (3, xf, yf)], dw_f32)
        dw_back_even.start()
        dx_next.wait_recv()

        def dx_last(cols, value):
            gx_ref[:, cols] = (dxa[:, cols] + dxf[:, cols].astype(F32) + value).astype(BF16)

        input_terms([(2, 2)], dx_last)
        part_a_odd.wait_recv()
        dw_back_odd.wait_recv()
        for k in range(3):
            gw_ref[k] = (dw0[k] + pa[k].astype(F32) + ca[k].astype(F32)).astype(BF16)
        for copy in (w_next, x_back, y_back, w_mate, part_a_even, w_last_back, dx_next, dw_back_even):
            copy.wait_send()

    @pl.when(odd)
    def _():
        forward(0, x_ref, y_ref, 0)
        w_mate.wait_recv()
        forward(1, x_ref, y_ref, 3)
        middle(0)
        middle(1)
        gathered(0)
        gathered(1)
        weight_terms([(1, x_ref, y_ref)], to_bf16(sp.at[0]))
        part_a_odd.start()
        w_next.wait_recv()
        w_last.start()
        w_next_back.start()
        forward(2, x_ref, y_ref, 1)
        weight_terms([(0, x_ref, y_ref)], to_f32(dw0))
        middle(2)
        gathered(2)
        part_a_even.wait_recv()

        def dw_sum(k, cols, value):
            sc[k, :, cols] = (value + pa[k, :, cols].astype(F32)).astype(BF16)

        weight_terms([(2, x_ref, y_ref)], dw_sum)
        dw_back_odd.start()
        input_terms([(0, 0), (1, 3), (2, 1)], dx_acc)
        w_last_back.wait_recv()
        forward(3, x_ref, y_ref, 2)
        middle(3)
        gathered(3)
        weight_terms([(3, x_ref, y_ref)], to_bf16(sp.at[1]))
        part_b.start()

        def dx_last(cols, value):
            gx_ref[:, cols] = (dxa[:, cols] + value).astype(BF16)

        input_terms([(3, 2)], dx_last)
        dw_back_even.wait_recv()
        for k in range(3):
            gw_ref[k] = (dw0[k] + ca[k].astype(F32)).astype(BF16)
        for copy in (part_a_odd, w_last, w_next_back, dw_back_odd, part_b):
            copy.wait_send()

    for st in range(4):
        for by in range(1, n_tensor):
            rs_copy(st, by).wait_send()
            ag_copy(st, by).wait_send()


def solution(mesh):
    n_section, n_tensor = mesh.shape["section"], mesh.shape["tensor"]

    def local(x, y, weights):
        tokens, depth = x.shape
        height = weights.shape[1]
        padded = -(-height // 128) * 128
        rows = tokens // n_tensor
        tile = min(depth, 512)
        vmem = pl.BlockSpec(memory_space=pltpu.VMEM)
        return pl.pallas_call(
            functools.partial(kernel, n_section, n_tensor, tile),
            out_shape=(
                jax.ShapeDtypeStruct((tokens, depth), BF16),
                jax.ShapeDtypeStruct((3, height, depth), BF16),
            ),
            in_specs=[vmem] * 3,
            out_specs=(vmem, vmem),
            scratch_shapes=[
                pltpu.VMEM((4, 3, padded, depth), BF16),
                pltpu.VMEM((tokens, depth), BF16),
                pltpu.VMEM((tokens, depth), BF16),
                pltpu.VMEM((4, tokens, 3 * padded), F32),
                pltpu.VMEM((4, tokens, 3 * padded), BF16),
                pltpu.VMEM((4, n_tensor - 1, rows, 3 * padded), BF16),
                pltpu.VMEM((4, tokens, 3 * padded), BF16),
                pltpu.VMEM((4, 3 * padded, tokens), BF16),
                pltpu.VMEM((3, height, depth), F32),
                pltpu.VMEM((tokens, depth), F32),
                pltpu.VMEM((3, height, depth), BF16),
                pltpu.VMEM((3, height, depth), BF16),
                pltpu.VMEM((3, height, depth), BF16),
                pltpu.VMEM((tokens, depth), BF16),
                pltpu.VMEM((2, 3, height, depth), BF16),
                pltpu.VMEM((3, height, depth), BF16),
                pltpu.VMEM((tokens, depth), BF16),
                pltpu.SemaphoreType.DMA((11,)),
                pltpu.SemaphoreType.DMA((11,)),
                pltpu.SemaphoreType.DMA((4, n_tensor - 1)),
                pltpu.SemaphoreType.DMA((4, n_tensor - 1)),
                pltpu.SemaphoreType.DMA((4, n_tensor - 1)),
                pltpu.SemaphoreType.DMA((4, n_tensor - 1)),
            ],
            compiler_params=pltpu.CompilerParams(
                collective_id=0, has_side_effects=True, vmem_limit_bytes=52 * 2**20
            ),
            cost_estimate=pl.CostEstimate(
                flops=2 * 8 * 4 * tokens * height * depth,
                bytes_accessed=2 * 2 * (3 * tokens * depth + 6 * height * depth),
                transcendentals=4 * tokens * height,
            ),
        )(x, y, weights)

    return jax.shard_map(
        local,
        mesh=mesh,
        in_specs=(P("section", "tensor"), P("section", "tensor"), P(None, "section", "tensor")),
        out_specs=(P("section", "tensor"), P(None, "section", "tensor")),
        check_vma=False,
    )
```

```python
import functools

import jax
import jax.numpy as jnp
from jax import lax
from jax.experimental import pallas as pl
from jax.experimental.pallas import tpu as pltpu
from jax.sharding import PartitionSpec as P

MESH = pl.DeviceIdType.MESH
F32 = jnp.float32
BF16 = jnp.bfloat16

W_MATE, W_NEXT, W_NEXT_BACK, W_LAST, W_LAST_BACK, X_BACK, Y_BACK, PART_A, PART_B, DW_BACK, DX_NEXT = range(11)

HALF = 64
LAST_EVEN, LAST_ODD, FIRST_EVEN, FIRST_ODD = 62, 63, 0, 1
ROUTES = {
    "next_1": (LAST_EVEN, 49, FIRST_ODD, 1, 1, 1),
    "next_2": (LAST_EVEN, 41, FIRST_ODD, 1, 2, 1),
    "last_1": (LAST_ODD, 33, FIRST_EVEN, 1, 1, 1),
    "last_2": (LAST_ODD, 25, FIRST_EVEN, 1, 2, 1),
    "dx_1": (LAST_EVEN, 49, FIRST_EVEN, 1, 6, 5),
    "dx_2": (LAST_EVEN, 41, FIRST_EVEN, 1, 11, 5),
    "x_1": (FIRST_EVEN, 15, LAST_EVEN, -1, 4, 6),
    "x_2": (FIRST_EVEN, 23, LAST_EVEN, -1, 10, 6),
    "y_1": (FIRST_EVEN, 31, LAST_EVEN, -1, 4, 6),
    "y_2": (FIRST_EVEN, 39, LAST_EVEN, -1, 10, 6),
    "dw_even_1": (FIRST_EVEN, 15, LAST_ODD, -1, 1, 1),
    "dw_even_2": (FIRST_EVEN, 39, LAST_ODD, -1, 2, 1),
    "dw_odd_1": (FIRST_ODD, 23, LAST_EVEN, -1, 1, 1),
    "dw_odd_2": (FIRST_ODD, 31, LAST_EVEN, -1, 2, 1),
}


def route_steps(name):
    sender, relay, receiver, halves = ROUTES[name][:4]
    return relay - sender + HALF * halves, receiver - relay


def route_greetings():
    found = {}
    for name, (sender, relay, receiver, *_) in ROUTES.items():
        there, on = route_steps(name)
        for place, by in ((sender, there), (relay, -there), (relay, on), (receiver, -on)):
            if by not in found.setdefault(place, []):
                found[place].append(by)
    return found


def dot_nt(a, b):
    return lax.dot_general(a, b, (((1,), (1,)), ((), ())), preferred_element_type=F32)


def dot_nn(a, b):
    return jnp.dot(a, b, preferred_element_type=F32)


def kernel(
    n_section, n_tensor, tile,
    x_ref, y_ref, wt_ref, gx_ref, gw_ref,
    w, xf, yf, part, rs_out, rs_in, ag, agt, dw0, dxa, pa, pb, ca, dxf, sp, sc, sx,
    hold_w, hold_dx, hold_xy, hold_dw,
    msg_s, msg_r, hold_s, hold_r, rs_s, rs_r, ag_s, ag_r, go,
):
    section, me_t = lax.axis_index("section"), lax.axis_index("tensor")
    even = lax.rem(section, 2) == 0
    odd = jnp.logical_not(even)
    tokens, depth = x_ref.shape
    height, padded = wt_ref.shape[1], w.shape[2]
    rows = tokens // n_tensor
    place = lax.rem(section, HALF)
    early = section < HALF

    def at(by):
        return (lax.rem(section + by + n_section, n_section), me_t)

    def peer(by):
        return (section, lax.rem(me_t + by, n_tensor))

    def rows_of(t):
        return pl.ds(pl.multiple_of(t * rows, rows), rows)

    def message(kind, src, dst, to):
        return pltpu.make_async_remote_copy(
            src_ref=src, dst_ref=dst, send_sem=msg_s.at[kind], recv_sem=msg_r.at[kind],
            device_id=to, device_id_type=MESH,
        )

    def slot(i):
        return w.at[i, :, pl.ds(0, height), :]

    def relayed(kind, name, src, hold, dst):
        there_by, on_by = route_steps(name)
        sem = list(ROUTES).index(name)
        unit = 1 if len(src.shape) == 3 else 16
        first, size = (n * unit for n in ROUTES[name][4:])
        part, hold = pl.ds(first, size), hold.at[pl.ds(0, size)]
        there = pltpu.make_async_remote_copy(
            src_ref=src.at[part], dst_ref=hold, send_sem=msg_s.at[kind], recv_sem=hold_r.at[sem],
            device_id=at(there_by), device_id_type=MESH,
        )
        on = pltpu.make_async_remote_copy(
            src_ref=hold, dst_ref=dst.at[part], send_sem=hold_s.at[sem], recv_sem=msg_r.at[kind],
            device_id=at(on_by), device_id_type=MESH,
        )
        return ROUTES[name][1], there, on

    def split(kind, name, src, hold, dst, to):
        names = [n for n in ROUTES if n.rsplit("_", 1)[0] == name]
        whole = src.shape[0]
        unit = 1 if len(src.shape) == 3 else 16
        size = whole - unit * sum(ROUTES[n][5] for n in names)
        part = pl.ds(0, size)
        first = message(kind, src.at[part], dst.at[part], to) if size else None
        return first, [relayed(kind, n, src, hold, dst) for n in names]

    def start_parts(*messages):
        for first, _ in messages:
            if first is not None:
                first.start()
        parts = [one for _, more in messages for one in more]

        @pl.when(me_t < n_tensor // 2)
        def _():
            for one in parts:
                one[1].start()

        @pl.when(me_t >= n_tensor // 2)
        def _():
            for one in parts[::-1]:
                one[1].start()

    def send(copy, at_place, parts):
        @pl.when(place != at_place)
        def _():
            copy.start()

        @pl.when(place == at_place)
        def _():
            start_parts(parts)

    def relay(copies, when=True):
        where, there, on = copies

        @pl.when((place == where) & when)
        def _():
            there.wait_recv()
            on.start()

    w_mate = message(W_MATE, wt_ref, slot(3), at(1))
    w_next = message(W_NEXT, wt_ref, slot(1), at(3))
    w_next_back = message(W_NEXT_BACK, slot(1), slot(1), at(-1))
    w_last = message(W_LAST, wt_ref, slot(2), at(1))
    w_last_back = message(W_LAST_BACK, slot(2), slot(2), at(1))
    x_back = message(X_BACK, x_ref, xf, at(-2))
    y_back = message(Y_BACK, y_ref, yf, at(-2))
    part_a_even = message(PART_A, sp.at[0], pa, at(1))
    part_a_odd = message(PART_A, sp.at[0], pa, at(-1))
    part_b = message(PART_B, sp.at[1], pb, at(-1))
    dw_back_even = message(DW_BACK, sc, ca, at(-1))
    dw_back_odd = message(DW_BACK, sc, ca, at(-3))
    dx_next = message(DX_NEXT, sx, dxf, at(2))

    next_parts = split(W_NEXT, "next", wt_ref, hold_w.at[0], slot(1), at(3))
    last_parts = split(W_LAST, "last", wt_ref, hold_w.at[1], slot(2), at(1))
    dx_parts = split(DX_NEXT, "dx", sx, hold_dx, dxf, at(2))
    x_parts = split(X_BACK, "x", x_ref, hold_xy.at[0], xf, at(-2))
    y_parts = split(Y_BACK, "y", y_ref, hold_xy.at[1], yf, at(-2))
    dwe_parts = split(DW_BACK, "dw_even", sc, hold_dw.at[0], ca, at(-1))
    dwo_parts = split(DW_BACK, "dw_odd", sc, hold_dw.at[1], ca, at(-3))
    all_parts = (next_parts, last_parts, dx_parts, x_parts, y_parts, dwe_parts, dwo_parts)

    def relay_all(messages, when=True):
        for _, more in messages:
            for one in more:
                relay(one, when)

    late = jnp.logical_not(early)

    barrier = pltpu.get_barrier_semaphore()

    def greet(to):
        pl.semaphore_signal(barrier, inc=1, device_id=to, device_id_type=MESH)

    for by in range(1, n_tensor):
        greet(peer(by))

    @pl.when(even)
    def _():
        for by in (1, -1, 3, -2, 2):
            greet(at(by))

    @pl.when(odd)
    def _():
        for by in (-1, 1, -3):
            greet(at(by))

    for where, others in route_greetings().items():

        @pl.when(place == where)
        def _(others=others):
            for by in others:
                greet(at(by))

    for i in range(4):
        w[i, :, height:, :] = jnp.zeros((3, padded - height, depth), BF16)
    w[0, :, :height, :] = wt_ref[...]

    expected = jnp.where(even, n_tensor - 1 + 5, n_tensor - 1 + 3)
    for where, others in route_greetings().items():
        expected = expected + jnp.where(place == where, len(others), 0)
    pl.semaphore_wait(barrier, expected)

    def rs_copy(st, by):
        return pltpu.make_async_remote_copy(
            src_ref=rs_out.at[st, rows_of(lax.rem(me_t + by, n_tensor))], dst_ref=rs_in.at[st, by - 1],
            send_sem=rs_s.at[st, by - 1], recv_sem=rs_r.at[st, by - 1],
            device_id=peer(by), device_id_type=MESH,
        )

    def ag_copy(st, by):
        return pltpu.make_async_remote_copy(
            src_ref=ag.at[st, rows_of(me_t)], dst_ref=ag.at[st, rows_of(me_t)],
            send_sem=ag_s.at[st, by - 1], recv_sem=ag_r.at[st, by - 1],
            device_id=peer(by), device_id_type=MESH,
        )

    def ag_arrival(st, by):
        src_t = lax.rem(me_t - by + n_tensor, n_tensor)
        return pltpu.make_async_remote_copy(
            src_ref=ag.at[st, rows_of(src_t)], dst_ref=ag.at[st, rows_of(src_t)],
            send_sem=ag_s.at[st, by - 1], recv_sem=ag_r.at[st, by - 1],
            device_id=peer(by), device_id_type=MESH,
        )

    def forward(st, x, y, i):
        gu = dot_nt(x[...], w[i, 0:2].reshape(2 * padded, depth))
        part[st, :, : 2 * padded] = gu
        rs_out[st, :, : 2 * padded] = gu.astype(BF16)
        d = dot_nt(y[...], w[i, 2])
        part[st, :, 2 * padded :] = d
        rs_out[st, :, 2 * padded :] = d.astype(BF16)
        for by in range(1, n_tensor):
            rs_copy(st, by).start()

    def middle(st):
        for by in range(1, n_tensor):
            rs_copy(st, by).wait_recv()
        own = rows_of(me_t)
        total = part[st, own, :]
        for by in range(1, n_tensor):
            total = total + rs_in[st, by - 1].astype(F32)
        g, u, dh = total[:, :padded], total[:, padded : 2 * padded], total[:, 2 * padded :]
        sig = jax.nn.sigmoid(g)
        silu = g * sig
        ag[st, own, :padded] = (dh * u * sig * (1.0 + g * (1.0 - sig))).astype(BF16)
        ag[st, own, padded : 2 * padded] = (dh * silu).astype(BF16)
        ag[st, own, 2 * padded :] = (silu * u).astype(BF16)
        for by in range(1, n_tensor):
            ag_copy(st, by).start()

    def gathered(st):
        for by in range(1, n_tensor):
            ag_arrival(st, by).wait_recv()
        agt[st] = ag[st].T

    def weight_terms(pairs, emit):
        for j in range(0, depth, tile):
            cols = pl.ds(j, tile)
            gu = sum(dot_nn(agt[st, : 2 * padded], x[:, cols]) for st, x, _ in pairs)
            emit(0, cols, gu[:height])
            emit(1, cols, gu[padded : padded + height])
            emit(2, cols, sum(dot_nn(agt[st, 2 * padded :], y[:, cols]) for st, _, y in pairs)[:height])

    def input_terms(pairs, emit):
        for j in range(0, depth, tile):
            cols = pl.ds(j, tile)
            emit(
                cols,
                sum(
                    dot_nn(ag[st, :, : 2 * padded], w[i, 0:2, :, cols].reshape(2 * padded, tile))
                    for st, i in pairs
                ),
            )

    def to_f32(ref):
        def emit(k, cols, value):
            ref[k, :, cols] = value

        return emit

    def to_bf16(ref):
        def emit(k, cols, value):
            ref[k, :, cols] = value.astype(BF16)

        return emit

    def dx_acc(cols, value):
        dxa[:, cols] = value

    @pl.when(even)
    def _():
        w_mate.start()
        send(w_next, LAST_EVEN, next_parts)

        @pl.when(place != FIRST_EVEN)
        def _():
            x_back.start()
            y_back.start()

        @pl.when(place == FIRST_EVEN)
        def _():
            start_parts(x_parts, y_parts)

        forward(0, x_ref, y_ref, 0)
        middle(0)
        gathered(0)
        weight_terms([(0, x_ref, y_ref)], to_f32(dw0))
        w_next.wait_send()
        pl.semaphore_signal(go, inc=1, device_id=at(1), device_id_type=MESH)
        w_next_back.wait_recv()
        forward(1, x_ref, y_ref, 1)
        middle(1)
        gathered(1)
        weight_terms([(1, x_ref, y_ref)], to_bf16(sp.at[0]))
        part_a_even.start()
        input_terms([(0, 0), (1, 1)], dx_acc)
        w_last.wait_recv()
        w_last_back.start()
        x_back.wait_recv()
        y_back.wait_recv()
        forward(3, xf, yf, 2)
        forward(2, x_ref, y_ref, 2)
        middle(3)
        middle(2)
        gathered(3)

        def dx_out(cols, value):
            sx[:, cols] = value.astype(BF16)

        input_terms([(3, 2)], dx_out)
        send(dx_next, LAST_EVEN, dx_parts)
        gathered(2)
        part_b.wait_recv()

        def dw_sum(k, cols, value):
            sc[k, :, cols] = (value + pb[k, :, cols].astype(F32)).astype(BF16)

        weight_terms([(2, x_ref, y_ref), (3, xf, yf)], dw_sum)
        send(dw_back_even, FIRST_EVEN, dwe_parts)
        dx_next.wait_recv()

        def dx_last(cols, value):
            gx_ref[:, cols] = (dxa[:, cols] + dxf[:, cols].astype(F32) + value).astype(BF16)

        input_terms([(2, 2)], dx_last)
        part_a_odd.wait_recv()
        dw_back_odd.wait_recv()
        for k in range(3):
            gw_ref[k] = (dw0[k] + pa[k].astype(F32) + ca[k].astype(F32)).astype(BF16)
        for copy in (x_back, y_back, w_mate, part_a_even, w_last_back, dx_next, dw_back_even):
            copy.wait_send()

    @pl.when(odd)
    def _():
        @pl.when(place == LAST_ODD)
        def _():
            start_parts(last_parts)

        forward(0, x_ref, y_ref, 0)
        w_mate.wait_recv()
        forward(1, x_ref, y_ref, 3)
        middle(0)
        middle(1)
        gathered(0)
        gathered(1)
        weight_terms([(1, x_ref, y_ref)], to_bf16(sp.at[0]))
        part_a_odd.start()
        relay_all((x_parts, y_parts, next_parts, last_parts), late)
        pl.semaphore_wait(go, 1)

        @pl.when(place != LAST_ODD)
        def _():
            w_last.start()

        w_next.wait_recv()

        w_next_back.start()
        forward(2, x_ref, y_ref, 1)
        weight_terms([(0, x_ref, y_ref)], to_f32(dw0))
        middle(2)
        gathered(2)
        part_a_even.wait_recv()

        def dw_sum(k, cols, value):
            sc[k, :, cols] = (value + pa[k, :, cols].astype(F32)).astype(BF16)

        weight_terms([(2, x_ref, y_ref)], dw_sum)
        send(dw_back_odd, FIRST_ODD, dwo_parts)
        input_terms([(0, 0), (1, 3), (2, 1)], dx_acc)
        relay_all((x_parts, y_parts, next_parts), early)
        w_last_back.wait_recv()
        forward(3, x_ref, y_ref, 2)
        middle(3)
        gathered(3)
        weight_terms([(3, x_ref, y_ref)], to_bf16(sp.at[1]))
        part_b.start()
        relay_all((last_parts,), early)
        relay_all((dx_parts, dwo_parts), late)

        def dx_last(cols, value):
            gx_ref[:, cols] = (dxa[:, cols] + value).astype(BF16)

        input_terms([(3, 2)], dx_last)
        relay_all((dx_parts, dwo_parts), early)
        relay_all((dwe_parts,))
        dw_back_even.wait_recv()
        for k in range(3):
            gw_ref[k] = (dw0[k] + ca[k].astype(F32)).astype(BF16)
        for copy in (part_a_odd, w_last, w_next_back, dw_back_odd, part_b):
            copy.wait_send()

    for _, more in all_parts:
        for copies in more:

            @pl.when(place == copies[0])
            def _(copies=copies):
                copies[2].wait_send()

    for st in range(4):
        for by in range(1, n_tensor):
            rs_copy(st, by).wait_send()
            ag_copy(st, by).wait_send()


def solution(mesh):
    n_section, n_tensor = mesh.shape["section"], mesh.shape["tensor"]

    def local(x, y, weights):
        tokens, depth = x.shape
        height = weights.shape[1]
        padded = -(-height // 128) * 128
        rows = tokens // n_tensor
        tile = min(depth, 512)
        vmem = pl.BlockSpec(memory_space=pltpu.VMEM)
        return pl.pallas_call(
            functools.partial(kernel, n_section, n_tensor, tile),
            out_shape=(
                jax.ShapeDtypeStruct((tokens, depth), BF16),
                jax.ShapeDtypeStruct((3, height, depth), BF16),
            ),
            in_specs=[vmem] * 3,
            out_specs=(vmem, vmem),
            scratch_shapes=[
                pltpu.VMEM((4, 3, padded, depth), BF16),
                pltpu.VMEM((tokens, depth), BF16),
                pltpu.VMEM((tokens, depth), BF16),
                pltpu.VMEM((4, tokens, 3 * padded), F32),
                pltpu.VMEM((4, tokens, 3 * padded), BF16),
                pltpu.VMEM((4, n_tensor - 1, rows, 3 * padded), BF16),
                pltpu.VMEM((4, tokens, 3 * padded), BF16),
                pltpu.VMEM((4, 3 * padded, tokens), BF16),
                pltpu.VMEM((3, height, depth), F32),
                pltpu.VMEM((tokens, depth), F32),
                pltpu.VMEM((3, height, depth), BF16),
                pltpu.VMEM((3, height, depth), BF16),
                pltpu.VMEM((3, height, depth), BF16),
                pltpu.VMEM((tokens, depth), BF16),
                pltpu.VMEM((2, 3, height, depth), BF16),
                pltpu.VMEM((3, height, depth), BF16),
                pltpu.VMEM((tokens, depth), BF16),
                pltpu.VMEM((2, 1, height, depth), BF16),
                pltpu.VMEM((tokens // 2, depth), BF16),
                pltpu.VMEM((2, tokens // 2, depth), BF16),
                pltpu.VMEM((2, 1, height, depth), BF16),
                pltpu.SemaphoreType.DMA((11,)),
                pltpu.SemaphoreType.DMA((11,)),
                pltpu.SemaphoreType.DMA((len(ROUTES),)),
                pltpu.SemaphoreType.DMA((len(ROUTES),)),
                pltpu.SemaphoreType.DMA((4, n_tensor - 1)),
                pltpu.SemaphoreType.DMA((4, n_tensor - 1)),
                pltpu.SemaphoreType.DMA((4, n_tensor - 1)),
                pltpu.SemaphoreType.DMA((4, n_tensor - 1)),
                pltpu.SemaphoreType.REGULAR,
            ],
            compiler_params=pltpu.CompilerParams(
                collective_id=0, has_side_effects=True, vmem_limit_bytes=52 * 2**20
            ),
            cost_estimate=pl.CostEstimate(
                flops=2 * 8 * 4 * tokens * height * depth,
                bytes_accessed=2 * 2 * (3 * tokens * depth + 6 * height * depth),
                transcendentals=4 * tokens * height,
            ),
        )(x, y, weights)

    return jax.shard_map(
        local,
        mesh=mesh,
        in_specs=(P("section", "tensor"), P("section", "tensor"), P(None, "section", "tensor")),
        out_specs=(P("section", "tensor"), P(None, "section", "tensor")),
        check_vma=False,
    )
```

```python
import functools

import jax
import jax.numpy as jnp
from jax import lax
from jax.experimental import pallas as pl
from jax.experimental.pallas import tpu as pltpu
from jax.sharding import PartitionSpec as P

MESH = pl.DeviceIdType.MESH
F32 = jnp.float32
BF16 = jnp.bfloat16

W_MATE, W_NEXT, W_NEXT_BACK, W_LAST, W_LAST_BACK, X_BACK, Y_BACK, PART_A, PART_B, DW_BACK, DX_NEXT = range(11)

HALF = 64
LAST_EVEN, LAST_ODD, FIRST_EVEN, FIRST_ODD = 62, 63, 0, 1
ROUTES = {
    "next_1": (LAST_EVEN, 49, FIRST_ODD, 1, 1, 1),
    "next_2": (LAST_EVEN, 41, FIRST_ODD, 1, 2, 1),
    "last_1": (LAST_ODD, 33, FIRST_EVEN, 1, 1, 1),
    "last_2": (LAST_ODD, 25, FIRST_EVEN, 1, 2, 1),
    "dx_1": (LAST_EVEN, 49, FIRST_EVEN, 1, 6, 5),
    "dx_2": (LAST_EVEN, 41, FIRST_EVEN, 1, 11, 5),
    "x_1": (FIRST_EVEN, 15, LAST_EVEN, -1, 4, 6),
    "x_2": (FIRST_EVEN, 23, LAST_EVEN, -1, 10, 6),
    "y_1": (FIRST_EVEN, 31, LAST_EVEN, -1, 4, 6),
    "y_2": (FIRST_EVEN, 39, LAST_EVEN, -1, 10, 6),
    "dw_even_1": (FIRST_EVEN, 15, LAST_ODD, -1, 1, 1),
    "dw_even_2": (FIRST_EVEN, 23, LAST_ODD, -1, 2, 1),
    "dw_odd_1": (FIRST_ODD, 31, LAST_EVEN, -1, 1, 1),
    "dw_odd_2": (FIRST_ODD, 39, LAST_EVEN, -1, 2, 1),
}


def route_steps(name):
    sender, relay, receiver, halves = ROUTES[name][:4]
    return relay - sender + HALF * halves, receiver - relay


def route_greetings():
    found = {}
    for name, (sender, relay, receiver, *_) in ROUTES.items():
        there, on = route_steps(name)
        for place, by in ((sender, there), (relay, -there), (relay, on), (receiver, -on)):
            if by not in found.setdefault(place, []):
                found[place].append(by)
    return found


def dot_nt(a, b):
    return lax.dot_general(a, b, (((1,), (1,)), ((), ())), preferred_element_type=F32)


def dot_nn(a, b):
    return jnp.dot(a, b, preferred_element_type=F32)


def kernel(
    n_section, n_tensor, tile,
    x_ref, y_ref, wt_ref, gx_ref, gw_ref,
    w, xf, yf, part, rs_out, rs_in, ag, agt, dw0, dxa, pa, pb, ca, dxf, sp, sc, sx,
    hold_w, hold_dx, hold_xy, hold_dw,
    msg_s, msg_r, hold_s, hold_r, rs_s, rs_r, ag_s, ag_r, go,
):
    section, me_t = lax.axis_index("section"), lax.axis_index("tensor")
    even = lax.rem(section, 2) == 0
    odd = jnp.logical_not(even)
    tokens, depth = x_ref.shape
    height, padded = wt_ref.shape[1], w.shape[2]
    rows = tokens // n_tensor
    place = lax.rem(section, HALF)
    early = section < HALF

    def at(by):
        return (lax.rem(section + by + n_section, n_section), me_t)

    def peer(by):
        return (section, lax.rem(me_t + by, n_tensor))

    def rows_of(t):
        return pl.ds(pl.multiple_of(t * rows, rows), rows)

    def message(kind, src, dst, to):
        return pltpu.make_async_remote_copy(
            src_ref=src, dst_ref=dst, send_sem=msg_s.at[kind], recv_sem=msg_r.at[kind],
            device_id=to, device_id_type=MESH,
        )

    def slot(i):
        return w.at[i, :, pl.ds(0, height), :]

    def relayed(kind, name, src, hold, dst):
        there_by, on_by = route_steps(name)
        sem = list(ROUTES).index(name)
        unit = 1 if len(src.shape) == 3 else 16
        first, size = (n * unit for n in ROUTES[name][4:])
        part, hold = pl.ds(first, size), hold.at[pl.ds(0, size)]
        there = pltpu.make_async_remote_copy(
            src_ref=src.at[part], dst_ref=hold, send_sem=msg_s.at[kind], recv_sem=hold_r.at[sem],
            device_id=at(there_by), device_id_type=MESH,
        )
        on = pltpu.make_async_remote_copy(
            src_ref=hold, dst_ref=dst.at[part], send_sem=hold_s.at[sem], recv_sem=msg_r.at[kind],
            device_id=at(on_by), device_id_type=MESH,
        )
        return ROUTES[name][1], there, on

    def split(kind, name, src, hold, dst, to):
        names = [n for n in ROUTES if n.rsplit("_", 1)[0] == name]
        whole = src.shape[0]
        unit = 1 if len(src.shape) == 3 else 16
        size = whole - unit * sum(ROUTES[n][5] for n in names)
        part = pl.ds(0, size)
        first = message(kind, src.at[part], dst.at[part], to) if size else None
        return first, [relayed(kind, n, src, hold, dst) for n in names]

    def start_parts(*messages):
        for first, _ in messages:
            if first is not None:
                first.start()
        parts = [one for _, more in messages for one in more]

        @pl.when(me_t < n_tensor // 2)
        def _():
            for one in parts:
                one[1].start()

        @pl.when(me_t >= n_tensor // 2)
        def _():
            for one in parts[::-1]:
                one[1].start()

    def send(copy, at_place, parts):
        @pl.when(place != at_place)
        def _():
            copy.start()

        @pl.when(place == at_place)
        def _():
            start_parts(parts)

    def relay(copies, when=True):
        where, there, on = copies

        @pl.when((place == where) & when)
        def _():
            there.wait_recv()
            on.start()

    w_mate = message(W_MATE, wt_ref, slot(3), at(1))
    w_next = message(W_NEXT, wt_ref, slot(1), at(3))
    w_next_back = message(W_NEXT_BACK, slot(1), slot(1), at(-1))
    w_last = message(W_LAST, wt_ref, slot(2), at(1))
    w_last_back = message(W_LAST_BACK, slot(2), slot(2), at(1))
    x_back = message(X_BACK, x_ref, xf, at(-2))
    y_back = message(Y_BACK, y_ref, yf, at(-2))
    part_a_even = message(PART_A, sp.at[0], pa, at(1))
    part_a_odd = message(PART_A, sp.at[0], pa, at(-1))
    part_b = message(PART_B, sp.at[1], pb, at(-1))
    dw_back_even = message(DW_BACK, sc, ca, at(-1))
    dw_back_odd = message(DW_BACK, sc, ca, at(-3))
    dx_next = message(DX_NEXT, sx, dxf, at(2))

    next_parts = split(W_NEXT, "next", wt_ref, hold_w.at[0], slot(1), at(3))
    last_parts = split(W_LAST, "last", wt_ref, hold_w.at[1], slot(2), at(1))
    dx_parts = split(DX_NEXT, "dx", sx, hold_dx, dxf, at(2))
    x_parts = split(X_BACK, "x", x_ref, hold_xy.at[0], xf, at(-2))
    y_parts = split(Y_BACK, "y", y_ref, hold_xy.at[1], yf, at(-2))
    dwe_parts = split(DW_BACK, "dw_even", sc, hold_dw.at[0], ca, at(-1))
    dwo_parts = split(DW_BACK, "dw_odd", sc, hold_dw.at[1], ca, at(-3))
    all_parts = (next_parts, last_parts, dx_parts, x_parts, y_parts, dwe_parts, dwo_parts)

    def relay_all(messages, when=True):
        for _, more in messages:
            for one in more:
                relay(one, when)

    late = jnp.logical_not(early)

    barrier = pltpu.get_barrier_semaphore()

    def greet(to):
        pl.semaphore_signal(barrier, inc=1, device_id=to, device_id_type=MESH)

    for by in range(1, n_tensor):
        greet(peer(by))

    @pl.when(even)
    def _():
        for by in (1, -1, 3, -2, 2):
            greet(at(by))

    @pl.when(odd)
    def _():
        for by in (-1, 1, -3):
            greet(at(by))

    for where, others in route_greetings().items():

        @pl.when(place == where)
        def _(others=others):
            for by in others:
                greet(at(by))

    for i in range(4):
        w[i, :, height:, :] = jnp.zeros((3, padded - height, depth), BF16)
    w[0, :, :height, :] = wt_ref[...]

    expected = jnp.where(even, n_tensor - 1 + 5, n_tensor - 1 + 3)
    for where, others in route_greetings().items():
        expected = expected + jnp.where(place == where, len(others), 0)
    pl.semaphore_wait(barrier, expected)

    def rs_copy(st, by):
        return pltpu.make_async_remote_copy(
            src_ref=rs_out.at[st, rows_of(lax.rem(me_t + by, n_tensor))], dst_ref=rs_in.at[st, by - 1],
            send_sem=rs_s.at[st, by - 1], recv_sem=rs_r.at[st, by - 1],
            device_id=peer(by), device_id_type=MESH,
        )

    def ag_copy(st, by):
        return pltpu.make_async_remote_copy(
            src_ref=ag.at[st, rows_of(me_t)], dst_ref=ag.at[st, rows_of(me_t)],
            send_sem=ag_s.at[st, by - 1], recv_sem=ag_r.at[st, by - 1],
            device_id=peer(by), device_id_type=MESH,
        )

    def ag_arrival(st, by):
        src_t = lax.rem(me_t - by + n_tensor, n_tensor)
        return pltpu.make_async_remote_copy(
            src_ref=ag.at[st, rows_of(src_t)], dst_ref=ag.at[st, rows_of(src_t)],
            send_sem=ag_s.at[st, by - 1], recv_sem=ag_r.at[st, by - 1],
            device_id=peer(by), device_id_type=MESH,
        )

    def forward(st, x, y, i):
        gu = dot_nt(x[...], w[i, 0:2].reshape(2 * padded, depth))
        part[st, :, : 2 * padded] = gu
        rs_out[st, :, : 2 * padded] = gu.astype(BF16)
        d = dot_nt(y[...], w[i, 2])
        part[st, :, 2 * padded :] = d
        rs_out[st, :, 2 * padded :] = d.astype(BF16)
        for by in range(1, n_tensor):
            rs_copy(st, by).start()

    def middle(st):
        for by in range(1, n_tensor):
            rs_copy(st, by).wait_recv()
        own = rows_of(me_t)
        total = part[st, own, :]
        for by in range(1, n_tensor):
            total = total + rs_in[st, by - 1].astype(F32)
        g, u, dh = total[:, :padded], total[:, padded : 2 * padded], total[:, 2 * padded :]
        sig = jax.nn.sigmoid(g)
        silu = g * sig
        ag[st, own, :padded] = (dh * u * sig * (1.0 + g * (1.0 - sig))).astype(BF16)
        ag[st, own, padded : 2 * padded] = (dh * silu).astype(BF16)
        ag[st, own, 2 * padded :] = (silu * u).astype(BF16)
        for by in range(1, n_tensor):
            ag_copy(st, by).start()

    def gathered(st):
        for by in range(1, n_tensor):
            ag_arrival(st, by).wait_recv()
        agt[st] = ag[st].T

    def weight_terms(pairs, emit):
        for j in range(0, depth, tile):
            cols = pl.ds(j, tile)
            gu = sum(dot_nn(agt[st, : 2 * padded], x[:, cols]) for st, x, _ in pairs)
            emit(0, cols, gu[:height])
            emit(1, cols, gu[padded : padded + height])
            emit(2, cols, sum(dot_nn(agt[st, 2 * padded :], y[:, cols]) for st, _, y in pairs)[:height])

    def input_terms(pairs, emit):
        for j in range(0, depth, tile):
            cols = pl.ds(j, tile)
            emit(
                cols,
                sum(
                    dot_nn(ag[st, :, : 2 * padded], w[i, 0:2, :, cols].reshape(2 * padded, tile))
                    for st, i in pairs
                ),
            )

    def to_f32(ref):
        def emit(k, cols, value):
            ref[k, :, cols] = value

        return emit

    def to_bf16(ref):
        def emit(k, cols, value):
            ref[k, :, cols] = value.astype(BF16)

        return emit

    def dx_acc(cols, value):
        dxa[:, cols] = value

    @pl.when(even)
    def _():
        w_mate.start()
        send(w_next, LAST_EVEN, next_parts)

        @pl.when(place != FIRST_EVEN)
        def _():
            x_back.start()
            y_back.start()

        @pl.when(place == FIRST_EVEN)
        def _():
            start_parts(x_parts, y_parts)

        forward(0, x_ref, y_ref, 0)
        middle(0)
        gathered(0)
        weight_terms([(0, x_ref, y_ref)], to_f32(dw0))
        w_next.wait_send()
        pl.semaphore_signal(go, inc=1, device_id=at(1), device_id_type=MESH)
        w_next_back.wait_recv()
        forward(1, x_ref, y_ref, 1)
        middle(1)
        w_last.wait_recv()
        w_last_back.start()
        x_back.wait_recv()
        y_back.wait_recv()
        forward(3, xf, yf, 2)
        forward(2, x_ref, y_ref, 2)
        gathered(1)
        weight_terms([(1, x_ref, y_ref)], to_bf16(sp.at[0]))
        part_a_even.start()
        middle(3)
        middle(2)
        input_terms([(0, 0), (1, 1)], dx_acc)
        gathered(3)

        def dx_out(cols, value):
            sx[:, cols] = value.astype(BF16)

        input_terms([(3, 2)], dx_out)
        send(dx_next, LAST_EVEN, dx_parts)
        gathered(2)
        part_b.wait_recv()

        def dw_sum(k, cols, value):
            sc[k, :, cols] = (value + pb[k, :, cols].astype(F32)).astype(BF16)

        weight_terms([(2, x_ref, y_ref), (3, xf, yf)], dw_sum)
        send(dw_back_even, FIRST_EVEN, dwe_parts)
        dx_next.wait_recv()

        def dx_last(cols, value):
            gx_ref[:, cols] = (dxa[:, cols] + dxf[:, cols].astype(F32) + value).astype(BF16)

        input_terms([(2, 2)], dx_last)
        part_a_odd.wait_recv()
        dw_back_odd.wait_recv()
        for k in range(3):
            gw_ref[k] = (dw0[k] + pa[k].astype(F32) + ca[k].astype(F32)).astype(BF16)
        for copy in (x_back, y_back, w_mate, part_a_even, w_last_back, dx_next, dw_back_even):
            copy.wait_send()

    @pl.when(odd)
    def _():
        @pl.when(place == LAST_ODD)
        def _():
            start_parts(last_parts)

        forward(0, x_ref, y_ref, 0)
        w_mate.wait_recv()
        forward(1, x_ref, y_ref, 3)
        middle(0)
        middle(1)
        gathered(0)
        gathered(1)
        weight_terms([(1, x_ref, y_ref)], to_bf16(sp.at[0]))
        part_a_odd.start()
        relay_all((x_parts, y_parts, next_parts, last_parts), late)
        pl.semaphore_wait(go, 1)

        @pl.when(place != LAST_ODD)
        def _():
            w_last.start()

        w_next.wait_recv()

        w_next_back.start()
        forward(2, x_ref, y_ref, 1)
        weight_terms([(0, x_ref, y_ref)], to_f32(dw0))
        relay_all((next_parts, last_parts), early)
        middle(2)
        relay_all((x_parts, y_parts), early)
        w_last_back.wait_recv()
        forward(3, x_ref, y_ref, 2)
        gathered(2)
        part_a_even.wait_recv()

        def dw_sum(k, cols, value):
            sc[k, :, cols] = (value + pa[k, :, cols].astype(F32)).astype(BF16)

        weight_terms([(2, x_ref, y_ref)], dw_sum)
        send(dw_back_odd, FIRST_ODD, dwo_parts)
        middle(3)
        input_terms([(0, 0), (1, 3), (2, 1)], dx_acc)
        gathered(3)
        weight_terms([(3, x_ref, y_ref)], to_bf16(sp.at[1]))
        part_b.start()
        relay_all((dx_parts, dwo_parts), late)

        def dx_last(cols, value):
            gx_ref[:, cols] = (dxa[:, cols] + value).astype(BF16)

        input_terms([(3, 2)], dx_last)
        relay_all((dx_parts, dwo_parts), early)
        relay_all((dwe_parts,))
        dw_back_even.wait_recv()
        for k in range(3):
            gw_ref[k] = (dw0[k] + ca[k].astype(F32)).astype(BF16)
        for copy in (part_a_odd, w_last, w_next_back, dw_back_odd, part_b):
            copy.wait_send()

    for _, more in all_parts:
        for copies in more:

            @pl.when(place == copies[0])
            def _(copies=copies):
                copies[2].wait_send()

    for st in range(4):
        for by in range(1, n_tensor):
            rs_copy(st, by).wait_send()
            ag_copy(st, by).wait_send()


def solution(mesh):
    n_section, n_tensor = mesh.shape["section"], mesh.shape["tensor"]

    def local(x, y, weights):
        tokens, depth = x.shape
        height = weights.shape[1]
        padded = -(-height // 128) * 128
        rows = tokens // n_tensor
        tile = min(depth, 512)
        vmem = pl.BlockSpec(memory_space=pltpu.VMEM)
        return pl.pallas_call(
            functools.partial(kernel, n_section, n_tensor, tile),
            out_shape=(
                jax.ShapeDtypeStruct((tokens, depth), BF16),
                jax.ShapeDtypeStruct((3, height, depth), BF16),
            ),
            in_specs=[vmem] * 3,
            out_specs=(vmem, vmem),
            scratch_shapes=[
                pltpu.VMEM((4, 3, padded, depth), BF16),
                pltpu.VMEM((tokens, depth), BF16),
                pltpu.VMEM((tokens, depth), BF16),
                pltpu.VMEM((4, tokens, 3 * padded), F32),
                pltpu.VMEM((4, tokens, 3 * padded), BF16),
                pltpu.VMEM((4, n_tensor - 1, rows, 3 * padded), BF16),
                pltpu.VMEM((4, tokens, 3 * padded), BF16),
                pltpu.VMEM((4, 3 * padded, tokens), BF16),
                pltpu.VMEM((3, height, depth), F32),
                pltpu.VMEM((tokens, depth), F32),
                pltpu.VMEM((3, height, depth), BF16),
                pltpu.VMEM((3, height, depth), BF16),
                pltpu.VMEM((3, height, depth), BF16),
                pltpu.VMEM((tokens, depth), BF16),
                pltpu.VMEM((2, 3, height, depth), BF16),
                pltpu.VMEM((3, height, depth), BF16),
                pltpu.VMEM((tokens, depth), BF16),
                pltpu.VMEM((2, 1, height, depth), BF16),
                pltpu.VMEM((tokens // 2, depth), BF16),
                pltpu.VMEM((2, tokens // 2, depth), BF16),
                pltpu.VMEM((2, 1, height, depth), BF16),
                pltpu.SemaphoreType.DMA((11,)),
                pltpu.SemaphoreType.DMA((11,)),
                pltpu.SemaphoreType.DMA((len(ROUTES),)),
                pltpu.SemaphoreType.DMA((len(ROUTES),)),
                pltpu.SemaphoreType.DMA((4, n_tensor - 1)),
                pltpu.SemaphoreType.DMA((4, n_tensor - 1)),
                pltpu.SemaphoreType.DMA((4, n_tensor - 1)),
                pltpu.SemaphoreType.DMA((4, n_tensor - 1)),
                pltpu.SemaphoreType.REGULAR,
            ],
            compiler_params=pltpu.CompilerParams(
                collective_id=0, has_side_effects=True, vmem_limit_bytes=52 * 2**20
            ),
            cost_estimate=pl.CostEstimate(
                flops=2 * 8 * 4 * tokens * height * depth,
                bytes_accessed=2 * 2 * (3 * tokens * depth + 6 * height * depth),
                transcendentals=4 * tokens * height,
            ),
        )(x, y, weights)

    return jax.shard_map(
        local,
        mesh=mesh,
        in_specs=(P("section", "tensor"), P("section", "tensor"), P(None, "section", "tensor")),
        out_specs=(P("section", "tensor"), P(None, "section", "tensor")),
        check_vma=False,
    )
```

```python
import functools

import jax
import jax.numpy as jnp
from jax import lax
from jax.experimental import pallas as pl
from jax.experimental.pallas import tpu as pltpu
from jax.sharding import PartitionSpec as P

MESH = pl.DeviceIdType.MESH
F32 = jnp.float32
BF16 = jnp.bfloat16

W_MATE, W_NEXT, W_NEXT_BACK, W_LAST, W_LAST_BACK, X_BACK, Y_BACK, PART_A, PART_B, DW_BACK, DX_NEXT = range(11)

HALF = 64
LAST_EVEN, LAST_ODD, FIRST_EVEN, FIRST_ODD = 62, 63, 0, 1
ROUTES = {
    "next_1": (LAST_EVEN, 49, FIRST_ODD, 1, 1, 1),
    "next_2": (LAST_EVEN, 41, FIRST_ODD, 1, 2, 1),
    "last_1": (LAST_ODD, 33, FIRST_EVEN, 1, 1, 1),
    "last_2": (LAST_ODD, 25, FIRST_EVEN, 1, 2, 1),
    "dx_1": (LAST_EVEN, 49, FIRST_EVEN, 1, 6, 5),
    "dx_2": (LAST_EVEN, 41, FIRST_EVEN, 1, 11, 5),
    "x_1": (FIRST_EVEN, 15, LAST_EVEN, -1, 4, 6),
    "x_2": (FIRST_EVEN, 23, LAST_EVEN, -1, 10, 6),
    "y_1": (FIRST_EVEN, 31, LAST_EVEN, -1, 4, 6),
    "y_2": (FIRST_EVEN, 39, LAST_EVEN, -1, 10, 6),
    "dw_even_1": (FIRST_EVEN, 15, LAST_ODD, -1, 4, 2),
    "dw_even_2": (FIRST_EVEN, 23, LAST_ODD, -1, 6, 1),
    "dw_odd_1": (FIRST_ODD, 31, LAST_EVEN, -1, 2, 3),
    "dw_odd_2": (FIRST_ODD, 39, LAST_EVEN, -1, 5, 2),
}


def route_steps(name):
    sender, relay, receiver, halves = ROUTES[name][:4]
    return relay - sender + HALF * halves, receiver - relay


def route_greetings():
    found = {}
    for name, (sender, relay, receiver, *_) in ROUTES.items():
        there, on = route_steps(name)
        for place, by in ((sender, there), (relay, -there), (relay, on), (receiver, -on)):
            if by not in found.setdefault(place, []):
                found[place].append(by)
    return found


def dot_nt(a, b):
    return lax.dot_general(a, b, (((1,), (1,)), ((), ())), preferred_element_type=F32)


def dot_nn(a, b):
    return jnp.dot(a, b, preferred_element_type=F32)


def kernel(
    n_section, n_tensor, tile,
    x_ref, y_ref, wt_ref, gx_ref, gw_ref,
    w, xf, yf, part, rs_out, rs_in, ag, agt, dw0, dxa, pa, pb, ca, dxf, sp, sc, sx,
    hold_w, hold_dx, hold_xy, hold_dw,
    msg_s, msg_r, hold_s, hold_r, rs_s, rs_r, ag_s, ag_r, go,
):
    section, me_t = lax.axis_index("section"), lax.axis_index("tensor")
    even = lax.rem(section, 2) == 0
    odd = jnp.logical_not(even)
    tokens, depth = x_ref.shape
    height, padded = wt_ref.shape[1], w.shape[2]
    rows = tokens // n_tensor
    place = lax.rem(section, HALF)
    early = section < HALF

    def at(by):
        return (lax.rem(section + by + n_section, n_section), me_t)

    def peer(by):
        return (section, lax.rem(me_t + by, n_tensor))

    def rows_of(t):
        return pl.ds(pl.multiple_of(t * rows, rows), rows)

    def message(kind, src, dst, to):
        return pltpu.make_async_remote_copy(
            src_ref=src, dst_ref=dst, send_sem=msg_s.at[kind], recv_sem=msg_r.at[kind],
            device_id=to, device_id_type=MESH,
        )

    def slot(i):
        return w.at[i, :, pl.ds(0, height), :]

    def rows_part(name, first, size):
        if name.startswith("dw"):
            return slice(None), pl.ds(16 * first, 16 * size)
        unit = 1 if name.startswith(("next", "last")) else 16
        return (pl.ds(unit * first, unit * size),)

    def relayed(kind, name, src, hold, dst):
        there_by, on_by = route_steps(name)
        sem = list(ROUTES).index(name)
        part = rows_part(name, *ROUTES[name][4:])
        hold = hold.at[rows_part(name, 0, ROUTES[name][5])]
        there = pltpu.make_async_remote_copy(
            src_ref=src.at[part], dst_ref=hold, send_sem=msg_s.at[kind], recv_sem=hold_r.at[sem],
            device_id=at(there_by), device_id_type=MESH,
        )
        on = pltpu.make_async_remote_copy(
            src_ref=hold, dst_ref=dst.at[part], send_sem=hold_s.at[sem], recv_sem=msg_r.at[kind],
            device_id=at(on_by), device_id_type=MESH,
        )
        return ROUTES[name][1], there, on

    def split(kind, name, src, hold, dst, to):
        names = [n for n in ROUTES if n.rsplit("_", 1)[0] == name]
        part = rows_part(name, 0, min(ROUTES[n][4] for n in names))
        first = message(kind, src.at[part], dst.at[part], to)
        return first, [relayed(kind, n, src, hold, dst) for n in names]

    def start_parts(*messages):
        for first, _ in messages:
            if first is not None:
                first.start()
        parts = [one for _, more in messages for one in more]

        @pl.when(me_t < n_tensor // 2)
        def _():
            for one in parts:
                one[1].start()

        @pl.when(me_t >= n_tensor // 2)
        def _():
            for one in parts[::-1]:
                one[1].start()

    def send(copy, at_place, parts):
        @pl.when(place != at_place)
        def _():
            copy.start()

        @pl.when(place == at_place)
        def _():
            start_parts(parts)

    def relay(copies, when=True):
        where, there, on = copies

        @pl.when((place == where) & when)
        def _():
            there.wait_recv()
            on.start()

    w_mate = message(W_MATE, wt_ref, slot(3), at(1))
    w_next = message(W_NEXT, wt_ref, slot(1), at(3))
    w_next_back = message(W_NEXT_BACK, slot(1), slot(1), at(-1))
    w_last = message(W_LAST, wt_ref, slot(2), at(1))
    w_last_back = message(W_LAST_BACK, slot(2), slot(2), at(1))
    x_back = message(X_BACK, x_ref, xf, at(-2))
    y_back = message(Y_BACK, y_ref, yf, at(-2))
    part_a_even = message(PART_A, sp.at[0], pa, at(1))
    part_a_odd = message(PART_A, sp.at[0], pa, at(-1))
    part_b = message(PART_B, sp.at[1], pb, at(-1))
    dw_back_even = message(DW_BACK, sc, ca, at(-1))
    dw_back_odd = message(DW_BACK, sc, ca, at(-3))
    dx_next = message(DX_NEXT, sx, dxf, at(2))

    next_parts = split(W_NEXT, "next", wt_ref, hold_w.at[0], slot(1), at(3))
    last_parts = split(W_LAST, "last", wt_ref, hold_w.at[1], slot(2), at(1))
    dx_parts = split(DX_NEXT, "dx", sx, hold_dx, dxf, at(2))
    x_parts = split(X_BACK, "x", x_ref, hold_xy.at[0], xf, at(-2))
    y_parts = split(Y_BACK, "y", y_ref, hold_xy.at[1], yf, at(-2))
    dwe_parts = split(DW_BACK, "dw_even", sc, hold_dw.at[0], ca, at(-1))
    dwo_parts = split(DW_BACK, "dw_odd", sc, hold_dw.at[1], ca, at(-3))
    all_parts = (next_parts, last_parts, dx_parts, x_parts, y_parts, dwe_parts, dwo_parts)

    def relay_all(messages, when=True):
        for _, more in messages:
            for one in more:
                relay(one, when)

    late = jnp.logical_not(early)

    barrier = pltpu.get_barrier_semaphore()

    def greet(to):
        pl.semaphore_signal(barrier, inc=1, device_id=to, device_id_type=MESH)

    for by in range(1, n_tensor):
        greet(peer(by))

    @pl.when(even)
    def _():
        for by in (1, -1, 3, -2, 2):
            greet(at(by))

    @pl.when(odd)
    def _():
        for by in (-1, 1, -3):
            greet(at(by))

    for where, others in route_greetings().items():

        @pl.when(place == where)
        def _(others=others):
            for by in others:
                greet(at(by))

    for i in range(4):
        w[i, :, height:, :] = jnp.zeros((3, padded - height, depth), BF16)
    w[0, :, :height, :] = wt_ref[...]

    expected = jnp.where(even, n_tensor - 1 + 5, n_tensor - 1 + 3)
    for where, others in route_greetings().items():
        expected = expected + jnp.where(place == where, len(others), 0)
    pl.semaphore_wait(barrier, expected)

    def rs_copy(st, by):
        return pltpu.make_async_remote_copy(
            src_ref=rs_out.at[st, rows_of(lax.rem(me_t + by, n_tensor))], dst_ref=rs_in.at[st, by - 1],
            send_sem=rs_s.at[st, by - 1], recv_sem=rs_r.at[st, by - 1],
            device_id=peer(by), device_id_type=MESH,
        )

    def ag_copy(st, by):
        return pltpu.make_async_remote_copy(
            src_ref=ag.at[st, rows_of(me_t)], dst_ref=ag.at[st, rows_of(me_t)],
            send_sem=ag_s.at[st, by - 1], recv_sem=ag_r.at[st, by - 1],
            device_id=peer(by), device_id_type=MESH,
        )

    def ag_arrival(st, by):
        src_t = lax.rem(me_t - by + n_tensor, n_tensor)
        return pltpu.make_async_remote_copy(
            src_ref=ag.at[st, rows_of(src_t)], dst_ref=ag.at[st, rows_of(src_t)],
            send_sem=ag_s.at[st, by - 1], recv_sem=ag_r.at[st, by - 1],
            device_id=peer(by), device_id_type=MESH,
        )

    def forward(st, x, y, i):
        gu = dot_nt(x[...], w[i, 0:2].reshape(2 * padded, depth))
        part[st, :, : 2 * padded] = gu
        rs_out[st, :, : 2 * padded] = gu.astype(BF16)
        d = dot_nt(y[...], w[i, 2])
        part[st, :, 2 * padded :] = d
        rs_out[st, :, 2 * padded :] = d.astype(BF16)
        for by in range(1, n_tensor):
            rs_copy(st, by).start()

    def middle(st):
        for by in range(1, n_tensor):
            rs_copy(st, by).wait_recv()
        own = rows_of(me_t)
        total = part[st, own, :]
        for by in range(1, n_tensor):
            total = total + rs_in[st, by - 1].astype(F32)
        g, u, dh = total[:, :padded], total[:, padded : 2 * padded], total[:, 2 * padded :]
        sig = jax.nn.sigmoid(g)
        silu = g * sig
        ag[st, own, :padded] = (dh * u * sig * (1.0 + g * (1.0 - sig))).astype(BF16)
        ag[st, own, padded : 2 * padded] = (dh * silu).astype(BF16)
        ag[st, own, 2 * padded :] = (silu * u).astype(BF16)
        for by in range(1, n_tensor):
            ag_copy(st, by).start()

    def gathered(st):
        for by in range(1, n_tensor):
            ag_arrival(st, by).wait_recv()
        agt[st] = ag[st].T

    def weight_terms(pairs, emit):
        for j in range(0, depth, tile):
            cols = pl.ds(j, tile)
            gu = sum(dot_nn(agt[st, : 2 * padded], x[:, cols]) for st, x, _ in pairs)
            emit(0, cols, gu[:height])
            emit(1, cols, gu[padded : padded + height])
            emit(2, cols, sum(dot_nn(agt[st, 2 * padded :], y[:, cols]) for st, _, y in pairs)[:height])

    def input_terms(pairs, emit):
        for j in range(0, depth, tile):
            cols = pl.ds(j, tile)
            emit(
                cols,
                sum(
                    dot_nn(ag[st, :, : 2 * padded], w[i, 0:2, :, cols].reshape(2 * padded, tile))
                    for st, i in pairs
                ),
            )

    def to_f32(ref):
        def emit(k, cols, value):
            ref[k, :, cols] = value

        return emit

    def to_bf16(ref):
        def emit(k, cols, value):
            ref[k, :, cols] = value.astype(BF16)

        return emit

    def dx_acc(cols, value):
        dxa[:, cols] = value

    @pl.when(even)
    def _():
        w_mate.start()
        send(w_next, LAST_EVEN, next_parts)

        @pl.when(place != FIRST_EVEN)
        def _():
            x_back.start()
            y_back.start()

        @pl.when(place == FIRST_EVEN)
        def _():
            start_parts(x_parts, y_parts)

        forward(0, x_ref, y_ref, 0)
        middle(0)
        gathered(0)
        weight_terms([(0, x_ref, y_ref)], to_f32(dw0))
        w_next.wait_send()
        pl.semaphore_signal(go, inc=1, device_id=at(1), device_id_type=MESH)
        w_next_back.wait_recv()
        forward(1, x_ref, y_ref, 1)
        middle(1)
        w_last.wait_recv()
        w_last_back.start()
        x_back.wait_recv()
        y_back.wait_recv()
        forward(3, xf, yf, 2)
        forward(2, x_ref, y_ref, 2)
        gathered(1)
        weight_terms([(1, x_ref, y_ref)], to_bf16(sp.at[0]))
        part_a_even.start()
        middle(3)
        middle(2)
        input_terms([(0, 0), (1, 1)], dx_acc)
        gathered(3)

        def dx_out(cols, value):
            sx[:, cols] = value.astype(BF16)

        input_terms([(3, 2)], dx_out)
        send(dx_next, LAST_EVEN, dx_parts)
        gathered(2)
        part_b.wait_recv()

        def dw_sum(k, cols, value):
            sc[k, :, cols] = (value + pb[k, :, cols].astype(F32)).astype(BF16)

        weight_terms([(2, x_ref, y_ref), (3, xf, yf)], dw_sum)
        send(dw_back_even, FIRST_EVEN, dwe_parts)
        dx_next.wait_recv()

        def dx_last(cols, value):
            gx_ref[:, cols] = (dxa[:, cols] + dxf[:, cols].astype(F32) + value).astype(BF16)

        input_terms([(2, 2)], dx_last)
        part_a_odd.wait_recv()
        dw_back_odd.wait_recv()
        for k in range(3):
            gw_ref[k] = (dw0[k] + pa[k].astype(F32) + ca[k].astype(F32)).astype(BF16)
        for copy in (x_back, y_back, w_mate, part_a_even, w_last_back, dx_next, dw_back_even):
            copy.wait_send()

    @pl.when(odd)
    def _():
        @pl.when(place == LAST_ODD)
        def _():
            start_parts(last_parts)

        forward(0, x_ref, y_ref, 0)
        w_mate.wait_recv()
        forward(1, x_ref, y_ref, 3)
        middle(0)
        middle(1)
        gathered(0)
        gathered(1)
        weight_terms([(1, x_ref, y_ref)], to_bf16(sp.at[0]))
        part_a_odd.start()
        relay_all((x_parts, y_parts, next_parts, last_parts), late)
        pl.semaphore_wait(go, 1)

        @pl.when(place != LAST_ODD)
        def _():
            w_last.start()

        w_next.wait_recv()

        w_next_back.start()
        forward(2, x_ref, y_ref, 1)
        weight_terms([(0, x_ref, y_ref)], to_f32(dw0))
        relay_all((next_parts, last_parts), early)
        middle(2)
        relay_all((x_parts, y_parts), early)
        w_last_back.wait_recv()
        forward(3, x_ref, y_ref, 2)
        gathered(2)
        part_a_even.wait_recv()

        def dw_sum(k, cols, value):
            sc[k, :, cols] = (value + pa[k, :, cols].astype(F32)).astype(BF16)

        weight_terms([(2, x_ref, y_ref)], dw_sum)
        send(dw_back_odd, FIRST_ODD, dwo_parts)
        middle(3)
        input_terms([(0, 0), (1, 3), (2, 1)], dx_acc)
        gathered(3)
        weight_terms([(3, x_ref, y_ref)], to_bf16(sp.at[1]))
        part_b.start()
        relay_all((dx_parts, dwo_parts), late)

        def dx_last(cols, value):
            gx_ref[:, cols] = (dxa[:, cols] + value).astype(BF16)

        input_terms([(3, 2)], dx_last)
        relay_all((dx_parts, dwo_parts), early)
        relay_all((dwe_parts,))
        dw_back_even.wait_recv()
        for k in range(3):
            gw_ref[k] = (dw0[k] + ca[k].astype(F32)).astype(BF16)
        for copy in (part_a_odd, w_last, w_next_back, dw_back_odd, part_b):
            copy.wait_send()

    for _, more in all_parts:
        for copies in more:

            @pl.when(place == copies[0])
            def _(copies=copies):
                copies[2].wait_send()

    for st in range(4):
        for by in range(1, n_tensor):
            rs_copy(st, by).wait_send()
            ag_copy(st, by).wait_send()


def solution(mesh):
    n_section, n_tensor = mesh.shape["section"], mesh.shape["tensor"]

    def local(x, y, weights):
        tokens, depth = x.shape
        height = weights.shape[1]
        padded = -(-height // 128) * 128
        rows = tokens // n_tensor
        tile = min(depth, 512)
        vmem = pl.BlockSpec(memory_space=pltpu.VMEM)
        return pl.pallas_call(
            functools.partial(kernel, n_section, n_tensor, tile),
            out_shape=(
                jax.ShapeDtypeStruct((tokens, depth), BF16),
                jax.ShapeDtypeStruct((3, height, depth), BF16),
            ),
            in_specs=[vmem] * 3,
            out_specs=(vmem, vmem),
            scratch_shapes=[
                pltpu.VMEM((4, 3, padded, depth), BF16),
                pltpu.VMEM((tokens, depth), BF16),
                pltpu.VMEM((tokens, depth), BF16),
                pltpu.VMEM((4, tokens, 3 * padded), F32),
                pltpu.VMEM((4, tokens, 3 * padded), BF16),
                pltpu.VMEM((4, n_tensor - 1, rows, 3 * padded), BF16),
                pltpu.VMEM((4, tokens, 3 * padded), BF16),
                pltpu.VMEM((4, 3 * padded, tokens), BF16),
                pltpu.VMEM((3, height, depth), F32),
                pltpu.VMEM((tokens, depth), F32),
                pltpu.VMEM((3, height, depth), BF16),
                pltpu.VMEM((3, height, depth), BF16),
                pltpu.VMEM((3, height, depth), BF16),
                pltpu.VMEM((tokens, depth), BF16),
                pltpu.VMEM((2, 3, height, depth), BF16),
                pltpu.VMEM((3, height, depth), BF16),
                pltpu.VMEM((tokens, depth), BF16),
                pltpu.VMEM((2, 1, height, depth), BF16),
                pltpu.VMEM((tokens // 2, depth), BF16),
                pltpu.VMEM((2, tokens // 2, depth), BF16),
                pltpu.VMEM((2, 3, 48, depth), BF16),
                pltpu.SemaphoreType.DMA((11,)),
                pltpu.SemaphoreType.DMA((11,)),
                pltpu.SemaphoreType.DMA((len(ROUTES),)),
                pltpu.SemaphoreType.DMA((len(ROUTES),)),
                pltpu.SemaphoreType.DMA((4, n_tensor - 1)),
                pltpu.SemaphoreType.DMA((4, n_tensor - 1)),
                pltpu.SemaphoreType.DMA((4, n_tensor - 1)),
                pltpu.SemaphoreType.DMA((4, n_tensor - 1)),
                pltpu.SemaphoreType.REGULAR,
            ],
            compiler_params=pltpu.CompilerParams(
                collective_id=0, has_side_effects=True, vmem_limit_bytes=52 * 2**20
            ),
            cost_estimate=pl.CostEstimate(
                flops=2 * 8 * 4 * tokens * height * depth,
                bytes_accessed=2 * 2 * (3 * tokens * depth + 6 * height * depth),
                transcendentals=4 * tokens * height,
            ),
        )(x, y, weights)

    return jax.shard_map(
        local,
        mesh=mesh,
        in_specs=(P("section", "tensor"), P("section", "tensor"), P(None, "section", "tensor")),
        out_specs=(P("section", "tensor"), P(None, "section", "tensor")),
        check_vma=False,
    )
```
